128 devices in a mesh: dp: 16 (over z, x), tile: 8 (over y, core).
Axes of the slice: x: 4, y: 4, z: 4, core: 2. Of those that a mesh axis runs over, the one named last changes fastest.
Arguments:
- frames: bfloat16 [64, 8, 64, 256], P('dp', 'tile'), may hold values from -6 to 6
- kernels: bfloat16 [64, 9, 256, 256], P('dp'), may hold values from -0.125 to 0.125
- experts: int32 [64, 8, 4], P('dp', 'tile'), may hold values from 0 to 63, as said below
- counts: int32 [64, 8], P('dp', 'tile'), may hold values from 2 to 4
- gate_weights: float32 [64, 8, 4], P('dp', 'tile'), may hold values from 0.25 to 1
- cotangent: bfloat16 [64, 8, 64, 256], P('dp', 'tile'), may hold values from -6 to 6
Outputs:
- frames_out: bfloat16 [64, 8, 64, 256], P('dp', 'tile')
- input_grad: bfloat16 [64, 8, 64, 256], P('dp', 'tile')
- gate_grad: float32 [64, 8, 4], P('dp', 'tile')
- kernel_grad: float32 [64, 9, 256, 256], P('dp', None, None, 'tile')
The draws below stay inside these ranges and needn't reach their ends.
Inputs may be any that keep to these rules, and one draw needn't show every extreme that they name: A tile's 4 experts have distinct values of id // 4. Among the 4 tiles of one device (frames d * 4 to (d + 1) * 4 - 1 at one tile index), each value of id // 4 is named by at most 2 tiles, by exactly 2 for some, and all its slots there name the same id. A tile uses its first counts slots; later slots are ignored.
All inputs are finite; a program needn't handle non-finite values.
Results may differ from the reference program's by a relative error of at most 0.005.
Values may be sent and summed in bfloat16 or wider, within the bound.
No kernel may reach another device: no remote copies, remote signals or barrier semaphores. Data moves between devices by JAX's collectives and lax.ppermute only.
A program may use at most 256 MiB of HBM per device.

```python
import jax
import jax.numpy as jnp
from jax import lax

CHANNELS = 256
EXP_DEV = 4
SLOTS = 4
FR_DEV = 4
CAP = 2
TILE_ROWS = 1
TILE_COLS = 64
EXPERTS = 64
BATCH = 64
HEIGHT = 8
N_DP = 16
N_TILE = 8


def draw_experts(key, part):
    groups = N_DP * N_TILE
    listed = FR_DEV * SLOTS // CAP
    stride = SLOTS // CAP
    first, second, third, fourth = jax.random.split(key, 4)
    specialist_order = jax.random.permutation(first, N_DP)
    affinity_increment = jnp.maximum(0, 3 - specialist_order)
    stochastic_perturbation = jax.random.randint(second, (groups, N_DP), 0, 4)
    order_keys = jax.random.split(third, groups)
    equality_resolver = jax.vmap(lambda single: jax.random.permutation(single, N_DP))(order_keys)
    specialist_affinity = (stochastic_perturbation + affinity_increment[None, :]) * N_DP + equality_resolver
    listing = lax.top_k(specialist_affinity, listed)[1]
    spots = (jnp.arange(FR_DEV)[:, None] * stride + jnp.arange(SLOTS)[None, :]) % listed
    owners = listing[:, spots]
    local_ids = jax.random.randint(fourth, (groups, N_DP), 0, EXP_DEV)
    taken = jnp.take_along_axis(local_ids, owners.reshape(groups, FR_DEV * SLOTS), axis=1).reshape(owners.shape)
    ids = (owners * EXP_DEV + taken).astype(jnp.int32)
    ids = ids.reshape(N_DP, N_TILE, FR_DEV, SLOTS).transpose(0, 2, 1, 3)
    return ids.reshape(N_DP * FR_DEV, N_TILE, SLOTS)


def set_ends(values, own_key, smallest, high):
    place = [jax.random.randint(jax.random.fold_in(own_key, axis), (), 0, length) for axis, length in enumerate(values.shape)]
    main_axis = values.shape.index(max(values.shape))
    next_to = place[:main_axis] + [(place[main_axis] + 1) % values.shape[main_axis]] + place[main_axis + 1:]
    return values.at[tuple(place)].set(smallest).at[tuple(next_to)].set(high)


def levels(own_key, shape, cuts, smallest, top_value):
    factor_of = 1.0
    for dim, shards_of in cuts:
        draws = jax.random.uniform(jax.random.fold_in(jax.random.fold_in(own_key, 6), dim), (shards_of,), jnp.float32, smallest / len(cuts), top_value / len(cuts))
        factor_of = factor_of * jnp.repeat(jnp.exp(draws), shape[dim] // shards_of).reshape((-1,) + (1,) * (len(shape) - 1 - dim))
    return factor_of


def bell_draw(key, shape, spread, most, cuts=(), held_as=jnp.bfloat16):
    drawn = jax.random.normal(key, shape, jnp.float32) * spread
    if len(cuts) > 0:
        drawn = levels(key, shape, cuts, -0.22, 0.18) * drawn
    return jnp.clip(drawn, min=-most, max=most).astype(held_as)


def setup_inputs(seed: int = 0) -> dict:
    seeds = jax.random.split(jax.random.key(seed), 7)
    return {
        "frames": bell_draw(seeds[0], (BATCH, HEIGHT, TILE_COLS, CHANNELS), 1.0, 6.0, ((0, 16), (1, 8))),
        "kernels": bell_draw(seeds[1], (EXPERTS, 9, CHANNELS, CHANNELS), (9 * CHANNELS) ** -0.5, 0.125, ((0, 16),)),
        "experts": draw_experts(jax.random.fold_in(seeds[6], 71), 0),
        "counts": set_ends(jax.random.randint(seeds[3], (BATCH, N_TILE), 2, SLOTS + 1), jax.random.fold_in(seeds[3], 1), 2, SLOTS).astype(jnp.int32),
        "gate_weights": jnp.clip(0.25 + 0.75 * jax.random.uniform(seeds[4], (BATCH, N_TILE, SLOTS), jnp.float32) ** levels(seeds[4], (BATCH, N_TILE, SLOTS), ((0, 16), (1, 8)), -0.2, 0.2), 0.25, 1.0),
        "cotangent": bell_draw(seeds[5], (BATCH, HEIGHT, TILE_COLS, CHANNELS), 1.0, 6.0, ((0, 16), (1, 8))),
    }


def convolve(window, kernel_weight):
    number_of_rows = window.shape[0] - 2
    columns = window.shape[1]
    widened = jnp.pad(window, ((0, 0), (1, 1), (0, 0)))
    total = jnp.zeros((number_of_rows * columns, kernel_weight.shape[2]), jnp.float32)
    for row_off in range(3):
        for col_off in range(3):
            patch = widened[row_off:row_off + number_of_rows, col_off:col_off + columns].reshape(number_of_rows * columns, -1)
            total = total + jnp.dot(patch, kernel_weight[3 * row_off + col_off], preferred_element_type=jnp.float32)
    return total.reshape(number_of_rows, columns, -1)


def transpose_conv(grad_out, kernel_weight):
    number_of_rows = grad_out.shape[0]
    columns = grad_out.shape[1]
    widened = jnp.pad(grad_out, ((2, 2), (1, 1), (0, 0)))
    total = jnp.zeros(((number_of_rows + 2) * columns, kernel_weight.shape[1]), jnp.float32)
    for row_off in range(3):
        for col_off in range(3):
            patch = widened[2 - row_off:4 - row_off + number_of_rows, 2 - col_off:2 - col_off + columns].reshape((number_of_rows + 2) * columns, -1)
            total = total + lax.dot_general(patch, kernel_weight[3 * row_off + col_off], (((1,), (1,)), ((), ())), preferred_element_type=jnp.float32)
    return total.reshape(number_of_rows + 2, columns, -1)


def kernel_terms(window, grad_out):
    number_of_rows = grad_out.shape[0]
    columns = grad_out.shape[1]
    widened = jnp.pad(window, ((0, 0), (1, 1), (0, 0)))
    flat_grad = grad_out.reshape(number_of_rows * columns, -1)
    pieces = []
    for row_off in range(3):
        for col_off in range(3):
            patch = widened[row_off:row_off + number_of_rows, col_off:col_off + columns].reshape(number_of_rows * columns, -1)
            pieces.append(lax.dot_general(patch, flat_grad, (((0,), (0,)), ((), ())), preferred_element_type=jnp.float32))
    return jnp.stack(pieces)


def activation(pre):
    squash = jax.nn.sigmoid(pre)
    return pre * squash, squash * (1.0 + pre * (1.0 - squash))


def reference(frames, kernels, experts, counts, gate_weights, cotangent):
    padded_frames = jnp.pad(frames, ((0, 0), (1, 1), (0, 0), (0, 0)))
    width = frames.shape[2]
    channels = frames.shape[3]

    def advance(carry, index):
        kernel_grad, grad_frame = carry
        frame_index = index // N_TILE
        place_index = index % N_TILE
        first_row = (place_index * TILE_ROWS).astype(jnp.int32)
        anchor = jnp.zeros((), jnp.int32)
        window = lax.dynamic_slice(padded_frames, (frame_index, first_row, anchor, anchor), (1, TILE_ROWS + 2, width, channels))[0]
        upstream = lax.dynamic_slice(cotangent, (frame_index, first_row, anchor, anchor), (1, TILE_ROWS, width, channels))[0].astype(jnp.float32)
        chosen = experts[frame_index, place_index]
        active_count = counts[frame_index, place_index]
        gate_row = gate_weights[frame_index, place_index]
        result = window[1:-1].astype(jnp.float32)
        rim_sum = jnp.zeros((TILE_ROWS + 2, width, channels), jnp.float32)
        gate_terms = []
        for slot_index in range(SLOTS):
            kernel_weight = kernels[chosen[slot_index]]
            masked = (slot_index < active_count).astype(jnp.float32)
            gate_scale = masked * gate_row[slot_index].astype(jnp.float32)
            pre = lax.optimization_barrier(convolve(window, kernel_weight).astype(jnp.bfloat16)).astype(jnp.float32)
            activated, slope = activation(pre)
            result = result + gate_scale * activated
            gate_terms.append(masked * jnp.sum(upstream * activated))
            grad_pre = (upstream * gate_scale * slope).astype(jnp.bfloat16)
            kernel_grad = kernel_grad.at[chosen[slot_index]].add(kernel_terms(window, grad_pre))
            rim_sum = rim_sum + lax.optimization_barrier(transpose_conv(grad_pre, kernel_weight).astype(jnp.bfloat16)).astype(jnp.float32)
        former = lax.dynamic_slice(grad_frame, (frame_index, first_row, anchor, anchor), (1, TILE_ROWS + 2, width, channels))
        grad_frame = lax.dynamic_update_slice(grad_frame, former + rim_sum[None], (frame_index, first_row, anchor, anchor))
        return (kernel_grad, grad_frame), (result.astype(jnp.bfloat16), jnp.stack(gate_terms))

    initial = (jnp.zeros((kernels.shape[0], 9, channels, channels), jnp.float32),
               jnp.zeros((frames.shape[0], frames.shape[1] + 2, width, channels), jnp.float32))
    position_list = jnp.arange(frames.shape[0] * N_TILE, dtype=jnp.int32)
    (kernel_grad, grad_frame), (tiles, gate_terms) = lax.scan(advance, initial, position_list)
    tiles = tiles.reshape(frames.shape[0], N_TILE, TILE_ROWS, width, channels)
    frames_out = tiles.reshape(frames.shape)
    input_grad = (cotangent.astype(jnp.float32) + grad_frame[:, 1:-1]).astype(jnp.bfloat16)
    gate_grad = gate_terms.reshape(frames.shape[0], N_TILE, SLOTS)
    return (frames_out, input_grad, gate_grad, kernel_grad)
```

```python
import functools

import jax
import jax.numpy as jnp
from jax import lax
from jax.experimental import pallas as pl
from jax.experimental.pallas import tpu as pltpu
from jax.sharding import PartitionSpec as P

DP = 16
TILES = 8
CAP = 2
ITEMS = DP * CAP
FRAMES = 4
SLOTS = 4
LOCAL = 4
W = 64
C = 256
PACK = 4
ROWS = PACK * W
MAX_GROUPS = 12
MIB = 2**20

SMEM = pl.BlockSpec(memory_space=pltpu.SMEM)
VMEM = pl.BlockSpec(memory_space=pltpu.VMEM)


def route_kernel(experts, counts, gates, meta, slot_frame, item_slot, used):
    def clear(o, carry):
        used[o] = 0
        slot_frame[2 * o] = -1
        slot_frame[2 * o + 1] = -1
        for k in range(8):
            meta[o, k] = 0.0
        return carry

    lax.fori_loop(0, DP, clear, 0)
    for f in range(FRAMES):
        for j in range(SLOTS):
            item_slot[f * SLOTS + j] = -1

            @pl.when(j < counts[f])
            def _():
                e = experts[f, j]
                o = e // LOCAL
                c = used[o]
                used[o] = c + 1
                slot_frame[CAP * o + c] = f
                item_slot[f * SLOTS + j] = CAP * o + c
                meta[o, 0] = (e - o * LOCAL).astype(jnp.float32)
                meta[o, 1 + c] = 1.0
                meta[o, 3 + c] = gates[f, j]


def route(experts, counts, gates):
    return pl.pallas_call(
        route_kernel,
        out_shape=(
            jax.ShapeDtypeStruct((DP, 8), jnp.float32),
            jax.ShapeDtypeStruct((ITEMS,), jnp.int32),
            jax.ShapeDtypeStruct((FRAMES * SLOTS,), jnp.int32),
        ),
        in_specs=[SMEM] * 3,
        out_specs=(SMEM,) * 3,
        scratch_shapes=[pltpu.SMEM((DP,), jnp.int32)],
        name="route",
    )(experts, counts, gates)


def pack_kernel(slot_frame, frames, above, below, cotangent, out):
    step = pl.program_id(0)
    for k in range(8):
        f = slot_frame[step * 8 + k]

        @pl.when(f >= 0)
        def _():
            out[k, 0] = above[f]
            out[k, 1] = frames[f]
            out[k, 2] = below[f]
            out[k, 3] = cotangent[f]


def pack(slot_frame, frames, above, below, cotangent):
    whole = pl.BlockSpec((FRAMES, W, C), lambda i, s: (0, 0, 0))
    return pl.pallas_call(
        pack_kernel,
        grid_spec=pltpu.PrefetchScalarGridSpec(
            num_scalar_prefetch=1,
            grid=(ITEMS // 8,),
            in_specs=[whole] * 4,
            out_specs=pl.BlockSpec((8, 4, W, C), lambda i, s: (i, 0, 0, 0)),
        ),
        out_shape=jax.ShapeDtypeStruct((ITEMS, 4, W, C), jnp.bfloat16),
        compiler_params=pltpu.CompilerParams(vmem_limit_bytes=24 * MIB),
        name="pack",
    )(slot_frame, frames, above, below, cotangent)


def list_kernel(meta, order, scale, group_expert, groups):
    def clear(p, carry):
        order[p] = -1
        scale[p] = 0.0
        return carry

    lax.fori_loop(0, MAX_GROUPS * PACK, clear, 0)
    first = jnp.int32(0)
    for e in range(LOCAL):

        def take(s, place, e=e):
            here = meta[s, 0] == float(e)
            for c in range(CAP):
                hit = here & (meta[s, 1 + c] > 0.5)

                @pl.when(hit)
                def _():
                    order[place] = CAP * s + c
                    scale[place] = meta[s, 3 + c]

                place = place + jnp.where(hit, 1, 0)
            return place

        last = lax.fori_loop(0, DP, take, first * PACK)
        size = (last - first * PACK + PACK - 1) // PACK

        def name(g, carry, e=e):
            group_expert[g] = e
            return carry

        lax.fori_loop(first, first + size, name, 0)
        first = first + size
    groups[0] = first


def make_list(meta):
    return pl.pallas_call(
        list_kernel,
        out_shape=(
            jax.ShapeDtypeStruct((MAX_GROUPS * PACK,), jnp.int32),
            jax.ShapeDtypeStruct((MAX_GROUPS * PACK,), jnp.float32),
            jax.ShapeDtypeStruct((MAX_GROUPS,), jnp.int32),
            jax.ShapeDtypeStruct((1,), jnp.int32),
        ),
        in_specs=[SMEM],
        out_specs=(SMEM,) * 4,
        name="item_list",
    )(meta)


def slope_of(pre):
    squash = jax.nn.sigmoid(pre)
    return squash * (1.0 + pre * (1.0 - squash))


def earlier(x, column):
    return jnp.where(column == 0, 0.0, pltpu.roll(x, 1, 0))


def later(x, column):
    return jnp.where(column == W - 1, 0.0, pltpu.roll(x, x.shape[0] - 1, 0))


def owner_kernel(
    order, scale, group_expert, groups, items, weights, flipped, back, grads, window, upstream, wide
):
    column = lax.broadcasted_iota(jnp.int32, (ROWS, C), 0) % W

    def group(g, carry):
        e = group_expert[g]
        for k in range(PACK):
            rows = pl.ds(k * W, W)
            item = order[g * PACK + k]
            there = item >= 0
            item = jnp.maximum(item, 0)

            @pl.when(there)
            def _():
                for r in range(3):
                    window[rows, r * C : (r + 1) * C] = items[item, r]
                upstream[rows, :] = items[item, 3].astype(jnp.float32) * scale[g * PACK + k]

            @pl.when(jnp.logical_not(there))
            def _():
                window[rows, :] = jnp.zeros((W, 3 * C), jnp.bfloat16)
                upstream[rows, :] = jnp.zeros((W, C), jnp.float32)

        patch = window[...]
        taps = [
            jnp.dot(patch, weights[e, :, b].reshape(3 * C, C), preferred_element_type=jnp.float32)
            for b in range(3)
        ]
        pre = (earlier(taps[0], column) + taps[1] + later(taps[2], column)).astype(jnp.bfloat16)
        grad = (upstream[...] * slope_of(pre.astype(jnp.float32))).astype(jnp.bfloat16)
        grads[g] = grad
        exact = grad.astype(jnp.float32)
        wide[:, 0:C] = later(exact, column).astype(jnp.bfloat16)
        wide[:, C : 2 * C] = grad
        wide[:, 2 * C : 3 * C] = earlier(exact, column).astype(jnp.bfloat16)
        rim = jnp.dot(wide[...], flipped[e], preferred_element_type=jnp.float32).astype(jnp.bfloat16)
        for k in range(PACK):
            item = order[g * PACK + k]

            @pl.when(item >= 0)
            def _():
                here = jnp.maximum(item, 0)
                back[here, 0] = pre[k * W : (k + 1) * W]
                for r in range(3):
                    back[here, 1 + r] = rim[k * W : (k + 1) * W, r * C : (r + 1) * C]

        return carry

    lax.fori_loop(0, groups[0], group, 0)


def owner(order, scale, group_expert, groups, items, weights, flipped):
    return pl.pallas_call(
        owner_kernel,
        out_shape=(
            jax.ShapeDtypeStruct((ITEMS, 4, W, C), jnp.bfloat16),
            jax.ShapeDtypeStruct((MAX_GROUPS, ROWS, C), jnp.bfloat16),
        ),
        in_specs=[SMEM] * 4 + [VMEM] * 3,
        out_specs=(VMEM, VMEM),
        scratch_shapes=[
            pltpu.VMEM((ROWS, 3 * C), jnp.bfloat16),
            pltpu.VMEM((ROWS, C), jnp.float32),
            pltpu.VMEM((ROWS, 3 * C), jnp.bfloat16),
        ],
        compiler_params=pltpu.CompilerParams(vmem_limit_bytes=48 * MIB),
        cost_estimate=pl.CostEstimate(
            flops=24 * 151_000_000, bytes_accessed=20_000_000, transcendentals=500_000
        ),
        name="owner",
    )(order, scale, group_expert, groups, items, weights, flipped)


def terms_kernel(order, group_expert, groups, items, grads, total, window, wide):
    column = lax.broadcasted_iota(jnp.int32, (ROWS, C), 0) % W
    total[...] = jnp.zeros_like(total)

    def group(g, carry):
        e = group_expert[g]
        for k in range(PACK):
            rows = pl.ds(k * W, W)
            item = order[g * PACK + k]

            @pl.when(item >= 0)
            def _():
                for r in range(3):
                    window[rows, r * C : (r + 1) * C] = items[jnp.maximum(item, 0), r]

            @pl.when(item < 0)
            def _():
                window[rows, :] = jnp.zeros((W, 3 * C), jnp.bfloat16)

        grad = grads[g]
        exact = grad.astype(jnp.float32)
        shifted = [later(exact, column), exact, earlier(exact, column)]
        patch = window[...]
        for b in range(3):
            part = jnp.dot(
                shifted[b].T.astype(jnp.bfloat16), patch, preferred_element_type=jnp.float32
            )
            for a in range(3):
                total[:, e, a, b] += part[:, a * C : (a + 1) * C].reshape(TILES, C // TILES, C)
        return carry

    lax.fori_loop(0, groups[0], group, 0)


def terms(order, group_expert, groups, items, grads):
    return pl.pallas_call(
        terms_kernel,
        out_shape=jax.ShapeDtypeStruct((TILES, LOCAL, 3, 3, C // TILES, C), jnp.float32),
        in_specs=[SMEM] * 3 + [VMEM] * 2,
        out_specs=VMEM,
        scratch_shapes=[
            pltpu.VMEM((ROWS, 3 * C), jnp.bfloat16),
            pltpu.VMEM((ROWS, 3 * C), jnp.bfloat16),
        ],
        compiler_params=pltpu.CompilerParams(vmem_limit_bytes=48 * MIB),
        cost_estimate=pl.CostEstimate(
            flops=24 * 75_500_000, bytes_accessed=15_000_000, transcendentals=0
        ),
        name="terms",
    )(order, group_expert, groups, items, grads)


def combine_kernel(item_slot, gates, got, frames, cotangent, out, inner, edges, gate_grad):
    for f in range(FRAMES):
        upstream = cotangent[f].astype(jnp.float32)
        out_acc = frames[f].astype(jnp.float32)
        rim = [jnp.zeros((W, C), jnp.float32) for _ in range(3)]
        for j in range(SLOTS):
            slot = item_slot[f * SLOTS + j]
            there = slot >= 0
            slot = jnp.maximum(slot, 0)
            block = jnp.where(there, got[slot], jnp.zeros((4, W, C), jnp.bfloat16)).astype(
                jnp.float32
            )
            activated = block[0] * jax.nn.sigmoid(block[0])
            out_acc = out_acc + gates[f, j] * activated
            gate_grad[f, j] = jnp.sum(upstream * activated)
            for r in range(3):
                rim[r] = rim[r] + block[1 + r]
        out[f] = out_acc.astype(jnp.bfloat16)
        inner[f] = upstream + rim[1]
        edges[0, f] = rim[0].astype(jnp.bfloat16)
        edges[1, f] = rim[2].astype(jnp.bfloat16)


def combine(item_slot, gates, got, frames, cotangent):
    return pl.pallas_call(
        combine_kernel,
        out_shape=(
            jax.ShapeDtypeStruct((FRAMES, W, C), jnp.bfloat16),
            jax.ShapeDtypeStruct((FRAMES, W, C), jnp.float32),
            jax.ShapeDtypeStruct((2, FRAMES, W, C), jnp.bfloat16),
            jax.ShapeDtypeStruct((FRAMES, SLOTS), jnp.float32),
        ),
        in_specs=[SMEM] * 2 + [VMEM] * 3,
        out_specs=(VMEM, VMEM, VMEM, SMEM),
        compiler_params=pltpu.CompilerParams(vmem_limit_bytes=24 * MIB),
        name="combine",
    )(item_slot, gates, got, frames, cotangent)


UP = [(i, i + 1) for i in range(TILES - 1)]
DOWN = [(i + 1, i) for i in range(TILES - 1)]


def shards(frames, kernels, experts, counts, gate_weights, cotangent):
    frames = frames[:, 0]
    cotangent = cotangent[:, 0]
    gates = gate_weights[:, 0]
    above = lax.ppermute(frames, "tile", UP)
    below = lax.ppermute(frames, "tile", DOWN)
    meta, slot_frame, item_slot = route(experts[:, 0], counts[:, 0], gates)
    asked = lax.all_to_all(meta, "dp", split_axis=0, concat_axis=0, tiled=True)
    outgoing = pack(slot_frame, frames, above, below, cotangent)
    items = lax.all_to_all(outgoing, "dp", split_axis=0, concat_axis=0, tiled=True)
    weights = kernels.reshape(LOCAL, 3, 3, C, C)
    flipped = weights.transpose(0, 2, 4, 1, 3).reshape(LOCAL, 3 * C, 3 * C)
    order, scale, group_expert, groups = make_list(asked)
    back, grads = owner(order, scale, group_expert, groups, items, weights, flipped)
    got = lax.all_to_all(back, "dp", split_axis=0, concat_axis=0, tiled=True)
    total = terms(order, group_expert, groups, items, grads)
    part = lax.psum_scatter(
        total.reshape(TILES, LOCAL * 9 * (C // TILES), C), "tile", scatter_dimension=0, tiled=True
    )
    kernel_grad = part.reshape(LOCAL, 9, C // TILES, C).transpose(0, 1, 3, 2)
    out, inner, edges, gate_grad = combine(item_slot, gates, got, frames, cotangent)
    from_below = lax.ppermute(edges[0], "tile", DOWN)
    from_above = lax.ppermute(edges[1], "tile", UP)
    input_grad = (
        inner + from_below.astype(jnp.float32) + from_above.astype(jnp.float32)
    ).astype(jnp.bfloat16)
    return (out[:, None], input_grad[:, None], gate_grad[:, None], kernel_grad)


def solution(mesh):
    return jax.shard_map(
        shards,
        mesh=mesh,
        in_specs=(
            P("dp", "tile", None, None),
            P("dp", None, None, None),
            P("dp", "tile", None),
            P("dp", "tile"),
            P("dp", "tile", None),
            P("dp", "tile", None, None),
        ),
        out_specs=(
            P("dp", "tile", None, None),
            P("dp", "tile", None, None),
            P("dp", "tile", None),
            P("dp", None, None, "tile"),
        ),
        check_vma=False,
    )
```

```python
import functools

import jax
import jax.numpy as jnp
from jax import lax
from jax.experimental import pallas as pl
from jax.experimental.pallas import tpu as pltpu
from jax.sharding import PartitionSpec as P

DP = 16
TILES = 8
CAP = 2
ITEMS = DP * CAP
FRAMES = 4
SLOTS = 4
LOCAL = 4
W = 64
C = 256
PACK = 4
ROWS = PACK * W
MAX_GROUPS = 7
MIB = 2**20
BLOCKS = W // 16
ITEM_BLOCKS = 4 * BLOCKS
KNOWN = 5

SMEM = pl.BlockSpec(memory_space=pltpu.SMEM)
VMEM = pl.BlockSpec(memory_space=pltpu.VMEM)
HBM = pl.BlockSpec(memory_space=pltpu.HBM)


def route_kernel(experts, counts, gates, frames, cotangent, item_slot, tags, half, used, known):
    for f in range(FRAMES):
        for r, source in ((1, frames), (3, cotangent)):
            half[f, r * BLOCKS : (r + 1) * BLOCKS] = source[f].reshape(BLOCKS, 16, C)

    def clear(o, carry):
        used[o] = 0
        for k in range(KNOWN):
            known[o, k] = 0.0
        return carry

    lax.fori_loop(0, DP, clear, 0)
    for f in range(FRAMES):
        for j in range(SLOTS):
            i = f * SLOTS + j
            item_slot[i] = -1

            @pl.when(j < counts[f])
            def _(f=f, j=j, i=i):
                e = experts[f, j]
                o = e // LOCAL
                place = used[o]
                used[o] = place + 1
                item_slot[i] = CAP * o + place
                known[o, 0] = (e - o * LOCAL).astype(jnp.float32)
                known[o, 1 + place] = 1.0
                known[o, 3 + place] = gates[f, j]

    lane = lax.broadcasted_iota(jnp.int32, (16, C), 1)
    line = lax.broadcasted_iota(jnp.int32, (16, C), 0)
    for o in range(DP):
        values = jnp.zeros((16, C), jnp.float32)
        for k in range(KNOWN):
            values = jnp.where(lane == k, known[o, k], values)
        high = values.astype(jnp.bfloat16).astype(jnp.float32)
        middle = (values - high).astype(jnp.bfloat16).astype(jnp.float32)
        low = values - high - middle
        tags[o] = jnp.where(
            line == 0, high, jnp.where(line == 1, middle, jnp.where(line == 2, low, 0.0))
        ).astype(jnp.bfloat16)


def route(experts, counts, gates, frames, cotangent):
    return pl.pallas_call(
        route_kernel,
        out_shape=(
            jax.ShapeDtypeStruct((FRAMES * SLOTS,), jnp.int32),
            jax.ShapeDtypeStruct((DP, 16, C), jnp.bfloat16),
            jax.ShapeDtypeStruct((FRAMES, ITEM_BLOCKS, 16, C), jnp.bfloat16),
        ),
        in_specs=[SMEM] * 3 + [VMEM] * 2,
        out_specs=(SMEM, VMEM, VMEM),
        scratch_shapes=[pltpu.SMEM((DP,), jnp.int32), pltpu.SMEM((DP, KNOWN), jnp.float32)],
        compiler_params=pltpu.CompilerParams(vmem_limit_bytes=8 * MIB),
        name="route",
    )(experts, counts, gates, frames, cotangent)


def pack_kernel(item_slot, tags, half, above, below, out_0, out_1, tiles, sems, tag_sems):
    def send_tile(i, act):
        slot = item_slot[i]
        for c, target in enumerate((out_0, out_1)):

            @pl.when((slot >= 0) & (slot % CAP == c))
            def _(c=c, target=target):
                copy = pltpu.make_async_copy(
                    tiles.at[i // SLOTS],
                    target.at[jnp.maximum(slot, 0) // CAP, pl.ds(0, ITEM_BLOCKS)],
                    sems.at[i],
                )
                copy.start() if act == "start" else copy.wait()

    def send_tags(o, act):
        copy = pltpu.make_async_copy(tags.at[o], out_0.at[o, ITEM_BLOCKS], tag_sems.at[o])
        copy.start() if act == "start" else copy.wait()

    for o in range(DP):
        send_tags(o, "start")
    for f in range(FRAMES):
        tiles[f] = half[f]
        for r, source in ((0, above), (2, below)):
            tiles[f, r * BLOCKS : (r + 1) * BLOCKS] = source[f].reshape(BLOCKS, 16, C)
        for j in range(SLOTS):
            send_tile(f * SLOTS + j, "start")
    for o in range(DP):
        send_tags(o, "wait")
    for i in range(FRAMES * SLOTS):
        send_tile(i, "wait")


def pack(item_slot, tags, half, above, below):
    return pl.pallas_call(
        pack_kernel,
        out_shape=(
            jax.ShapeDtypeStruct((DP, ITEM_BLOCKS + 1, 16, C), jnp.bfloat16),
            jax.ShapeDtypeStruct((DP, ITEM_BLOCKS, 16, C), jnp.bfloat16),
        ),
        in_specs=[SMEM] + [VMEM] * 4,
        out_specs=(HBM, HBM),
        scratch_shapes=[
            pltpu.VMEM((FRAMES, ITEM_BLOCKS, 16, C), jnp.bfloat16),
            pltpu.SemaphoreType.DMA((FRAMES * SLOTS,)),
            pltpu.SemaphoreType.DMA((DP,)),
        ],
        compiler_params=pltpu.CompilerParams(vmem_limit_bytes=8 * MIB),
        name="pack",
    )(item_slot, tags, half, above, below)


def list_kernel(meta, *refs):
    found, size = refs[4 * CAP :]
    for c in range(CAP):
        order, scale, group_expert, groups = refs[4 * c : 4 * c + 4]

        def clear(p, carry, order=order, scale=scale):
            order[p] = -1
            scale[p] = 0.0
            return carry

        lax.fori_loop(0, MAX_GROUPS * PACK, clear, 0)
        for e in range(LOCAL):
            size[e] = 0

        def source(s, carry, c=c):
            @pl.when(meta[s, 1 + c] > 0.5)
            def _():
                e = meta[s, 0].astype(jnp.int32)
                n = size[e]
                found[e, n] = s
                size[e] = n + 1

            return carry

        lax.fori_loop(0, DP, source, 0)
        first = jnp.int32(0)
        for e in range(LOCAL):

            def copy(n, carry, e=e, c=c, order=order, scale=scale):
                s = found[e, n]
                order[carry + n] = s
                scale[carry + n] = meta[s, 3 + c]
                return carry

            lax.fori_loop(0, size[e], copy, first * PACK)
            last = first + (size[e] + PACK - 1) // PACK

            def name(g, carry, e=e, group_expert=group_expert):
                group_expert[g] = e
                return carry

            lax.fori_loop(first, last, name, 0)
            first = last
        groups[0] = first


def make_lists(meta):
    one = (
        jax.ShapeDtypeStruct((MAX_GROUPS * PACK,), jnp.int32),
        jax.ShapeDtypeStruct((MAX_GROUPS * PACK,), jnp.float32),
        jax.ShapeDtypeStruct((MAX_GROUPS,), jnp.int32),
        jax.ShapeDtypeStruct((1,), jnp.int32),
    )
    made = pl.pallas_call(
        list_kernel,
        out_shape=one * CAP,
        in_specs=[SMEM],
        out_specs=(SMEM,) * (4 * CAP),
        scratch_shapes=[
            pltpu.SMEM((LOCAL, DP), jnp.int32),
            pltpu.SMEM((LOCAL,), jnp.int32),
        ],
        name="item_lists",
    )(meta)
    return [made[4 * c : 4 * c + 4] for c in range(CAP)]


def slope_of(pre):
    squash = jax.nn.sigmoid(pre)
    return squash * (1.0 + pre * (1.0 - squash))


def earlier(x, column):
    return jnp.where(column == 0, 0.0, pltpu.roll(x, 1, 0))


def later(x, column):
    return jnp.where(column == W - 1, 0.0, pltpu.roll(x, x.shape[0] - 1, 0))


def row_of(items, item, r):
    return items[jnp.maximum(item, 0), r * BLOCKS : (r + 1) * BLOCKS].reshape(W, C)


def owner_kernel(place, order, scale, group_expert, groups, items, weights, *refs):
    if place == 0:
        back, pre_out, grads, window, upstream = refs
    else:
        other_pre, back, grads, window, upstream = refs
        pre_out = None
        back[:, 4] = other_pre[...]
    column = lax.broadcasted_iota(jnp.int32, (ROWS, C), 0) % W

    def group(g, carry):
        e = group_expert[g]
        for k in range(PACK):
            rows = pl.ds(k * W, W)
            item = order[g * PACK + k]

            @pl.when(item >= 0)
            def _():
                for r in range(3):
                    window[rows, r * C : (r + 1) * C] = row_of(items, item, r)
                upstream[rows, :] = row_of(items, item, 3).astype(jnp.float32) * scale[g * PACK + k]

            @pl.when(item < 0)
            def _():
                window[rows, :] = jnp.zeros((W, 3 * C), jnp.bfloat16)
                upstream[rows, :] = jnp.zeros((W, C), jnp.float32)

        patch = window[...]
        taps = [
            jnp.dot(patch, weights[e, :, b].reshape(3 * C, C), preferred_element_type=jnp.float32)
            for b in range(3)
        ]
        pre = (earlier(taps[0], column) + taps[1] + later(taps[2], column)).astype(jnp.bfloat16)
        grad = (upstream[...] * slope_of(pre.astype(jnp.float32))).astype(jnp.bfloat16)
        grads[g] = grad
        exact = grad.astype(jnp.float32)
        shifted = [
            later(exact, column).astype(jnp.bfloat16),
            grad,
            earlier(exact, column).astype(jnp.bfloat16),
        ]
        rims = [
            sum(
                lax.dot_general(
                    shifted[b],
                    weights[e, a, b],
                    (((1,), (1,)), ((), ())),
                    preferred_element_type=jnp.float32,
                )
                for b in range(3)
            ).astype(jnp.bfloat16)
            for a in range(3)
        ]
        for k in range(PACK):
            item = order[g * PACK + k]

            @pl.when(item >= 0)
            def _(k=k):
                here = jnp.maximum(item, 0)
                if pre_out is None:
                    back[here, 3] = pre[k * W : (k + 1) * W]
                else:
                    pre_out[here] = pre[k * W : (k + 1) * W]
                for r in range(3):
                    back[here, r] = rims[r][k * W : (k + 1) * W]

        return carry

    lax.fori_loop(0, groups[0], group, 0)


def owner(order, scale, group_expert, groups, items, weights, other_pre=None):
    rows = lambda *n: jax.ShapeDtypeStruct((DP, *n, W, C), jnp.bfloat16)
    more = [] if other_pre is None else [other_pre]
    made = [rows(5)] if more else [rows(3), rows()]
    made.append(jax.ShapeDtypeStruct((MAX_GROUPS, ROWS, C), jnp.bfloat16))
    return pl.pallas_call(
        functools.partial(owner_kernel, len(more)),
        out_shape=made,
        in_specs=[SMEM] * 4 + [VMEM] * (2 + len(more)),
        out_specs=[VMEM] * len(made),
        scratch_shapes=[
            pltpu.VMEM((ROWS, 3 * C), jnp.bfloat16),
            pltpu.VMEM((ROWS, C), jnp.float32),
        ],
        compiler_params=pltpu.CompilerParams(vmem_limit_bytes=16 * MIB),
        cost_estimate=pl.CostEstimate(
            flops=8_000_000_000, bytes_accessed=16_000_000, transcendentals=500_000
        ),
        name="owner",
    )(order, scale, group_expert, groups, items, weights, *more)


def shifted_products(g, order, items, grads, window):
    column = lax.broadcasted_iota(jnp.int32, (ROWS, C), 0) % W
    for k in range(PACK):
        rows = pl.ds(k * W, W)
        item = order[g * PACK + k]

        @pl.when(item >= 0)
        def _():
            for r in range(3):
                window[rows, r * C : (r + 1) * C] = row_of(items, item, r)

        @pl.when(item < 0)
        def _():
            window[rows, :] = jnp.zeros((W, 3 * C), jnp.bfloat16)

    exact = grads[g].astype(jnp.float32)
    patch = window[...]
    for b, x in enumerate((later(exact, column), exact, earlier(exact, column))):
        part = jnp.dot(x.T.astype(jnp.bfloat16), patch, preferred_element_type=jnp.float32)
        for a in range(3):
            yield 3 * a + b, part[:, a * C : (a + 1) * C].reshape(TILES, C // TILES, C)


def groups_before(e, group_expert, groups):
    return lax.fori_loop(
        0, groups[0], lambda g, n: n + jnp.where(group_expert[g] < e, 1, 0), jnp.int32(0)
    )


def terms_kernel(fresh, order, group_expert, groups, items, grads, *refs):
    if fresh:
        total, sums, window, sems = refs
    else:
        before, total, sums, window, sems, so_far, load_sems = refs

    def copy(e):
        return pltpu.make_async_copy(sums.at[e % 2], total.at[:, e], sems.at[e])

    def load(e):
        return pltpu.make_async_copy(before.at[:, e], so_far.at[:, e], load_sems.at[e])

    if not fresh:
        for e in range(LOCAL):
            load(e).start()
    for e in range(LOCAL):
        begin = groups_before(e, group_expert, groups)
        end = groups_before(e + 1, group_expert, groups)
        if e >= 2:
            copy(e - 2).wait()
        if not fresh:
            load(e).wait()

        def group(g, carry, e=e, begin=begin):
            for tap, part in shifted_products(g, order, items, grads, window):

                @pl.when(g == begin)
                def _(tap=tap, part=part):
                    sums[e % 2, :, tap] = part if fresh else so_far[:, e, tap] + part

                @pl.when(g != begin)
                def _(tap=tap, part=part):
                    sums[e % 2, :, tap] += part

            return carry

        lax.fori_loop(begin, end, group, 0)

        @pl.when(end == begin)
        def _(e=e):
            sums[e % 2] = (
                jnp.zeros((TILES, 9, C // TILES, C), jnp.float32) if fresh else so_far[:, e]
            )

        copy(e).start()
    for e in (LOCAL - 2, LOCAL - 1):
        copy(e).wait()


def terms(order, group_expert, groups, items, grads, so_far=None):
    fresh = so_far is None
    made = (TILES, LOCAL, 9, C // TILES, C)
    scratch = [
        pltpu.VMEM((2, TILES, 9, C // TILES, C), jnp.float32),
        pltpu.VMEM((ROWS, 3 * C), jnp.bfloat16),
        pltpu.SemaphoreType.DMA((LOCAL,)),
    ]
    if not fresh:
        scratch += [pltpu.VMEM(made, jnp.float32), pltpu.SemaphoreType.DMA((LOCAL,))]
    return pl.pallas_call(
        functools.partial(terms_kernel, fresh),
        out_shape=jax.ShapeDtypeStruct(made, jnp.float32),
        in_specs=[SMEM] * 3 + [VMEM] * 2 + ([] if fresh else [HBM]),
        out_specs=HBM,
        scratch_shapes=scratch,
        compiler_params=pltpu.CompilerParams(vmem_limit_bytes=48 * MIB),
        cost_estimate=pl.CostEstimate(
            flops=4_000_000_000, bytes_accessed=15_000_000, transcendentals=0
        ),
        name="first_terms" if fresh else "last_terms",
    )(order, group_expert, groups, items, grads, *([] if fresh else [so_far]))


def gathered(item_slot, places, add):
    for f in range(FRAMES):
        for j in range(SLOTS):
            slot = item_slot[f * SLOTS + j]
            for place in places:

                @pl.when((slot >= 0) & (slot % CAP == place))
                def _(f=f, j=j, slot=slot, place=place):
                    add(f, j, jnp.maximum(slot, 0) // CAP, place)


def first_kernel(item_slot, got, cotangent, sums):
    sums[0] = jnp.zeros((FRAMES, W, C), jnp.float32)
    sums[1] = cotangent[...].astype(jnp.float32)
    sums[2] = jnp.zeros((FRAMES, W, C), jnp.float32)

    def add(f, j, o, place):
        for r in range(3):
            sums[r, f] += got[o, r].astype(jnp.float32)

    gathered(item_slot, (0,), add)


def last_kernel(item_slot, gates, got, frames, cotangent, so_far, out, inner, edges, gate_grad, sums, total):
    sums[...] = so_far[...]
    total[...] = frames[...].astype(jnp.float32)
    for f in range(FRAMES):
        for j in range(SLOTS):
            gate_grad[f, j] = 0.0

    def add(f, j, o, place):
        pre = got[o, 4 - place].astype(jnp.float32)
        activated = pre * jax.nn.sigmoid(pre)
        total[f] += gates[f, j] * activated
        gate_grad[f, j] = jnp.sum(cotangent[f].astype(jnp.float32) * activated)
        if place == 1:
            for r in range(3):
                sums[r, f] += got[o, r].astype(jnp.float32)

    gathered(item_slot, (0, 1), add)
    out[...] = total[...].astype(jnp.bfloat16)
    inner[...] = sums[1]
    edges[0] = sums[0].astype(jnp.bfloat16)
    edges[1] = sums[2].astype(jnp.bfloat16)


def combine_first(item_slot, got, cotangent):
    return pl.pallas_call(
        first_kernel,
        out_shape=jax.ShapeDtypeStruct((3, FRAMES, W, C), jnp.float32),
        in_specs=[SMEM] + [VMEM] * 2,
        out_specs=VMEM,
        compiler_params=pltpu.CompilerParams(vmem_limit_bytes=12 * MIB),
        name="combine_first",
    )(item_slot, got, cotangent)


def combine_last(item_slot, gates, got, frames, cotangent, so_far):
    return pl.pallas_call(
        last_kernel,
        out_shape=(
            jax.ShapeDtypeStruct((FRAMES, W, C), jnp.bfloat16),
            jax.ShapeDtypeStruct((FRAMES, W, C), jnp.float32),
            jax.ShapeDtypeStruct((2, FRAMES, W, C), jnp.bfloat16),
            jax.ShapeDtypeStruct((FRAMES, SLOTS), jnp.float32),
        ),
        in_specs=[SMEM] * 2 + [VMEM] * 4,
        out_specs=(VMEM, VMEM, VMEM, SMEM),
        scratch_shapes=[
            pltpu.VMEM((3, FRAMES, W, C), jnp.float32),
            pltpu.VMEM((FRAMES, W, C), jnp.float32),
        ],
        compiler_params=pltpu.CompilerParams(vmem_limit_bytes=12 * MIB),
        name="combine_last",
    )(item_slot, gates, got, frames, cotangent, so_far)


UP = [(i, i + 1) for i in range(TILES - 1)]
DOWN = [(i + 1, i) for i in range(TILES - 1)]


def exchange(x):
    return lax.all_to_all(x, "dp", split_axis=0, concat_axis=0, tiled=True)


def shards(frames, kernels, experts, counts, gate_weights, cotangent):
    frames = frames[:, 0]
    cotangent = cotangent[:, 0]
    gates = gate_weights[:, 0]
    above = lax.ppermute(frames, "tile", UP)
    below = lax.ppermute(frames, "tile", DOWN)
    item_slot, tags, half = route(experts[:, 0], counts[:, 0], gates, frames, cotangent)
    outgoing = list(pack(item_slot, tags, half, above, below))
    items = [exchange(outgoing[0])]
    items[0], outgoing[1] = lax.optimization_barrier((items[0], outgoing[1]))
    items.append(exchange(outgoing[1]))
    meta = jnp.sum(items[0][:, ITEM_BLOCKS, :3, :KNOWN].astype(jnp.float32), axis=1)
    weights = kernels.reshape(LOCAL, 3, 3, C, C)
    lists = make_lists(meta)
    (order_0, scale, *of_groups), (order_1, scale_1, *of_groups_1) = lists
    back, pre, grads = owner(order_0, scale, *of_groups, items[0], weights)
    total = terms(order_0, *of_groups, items[0], grads)
    back, total = lax.optimization_barrier((back, total))
    got = exchange(back)
    rest, grads = owner(order_1, scale_1, *of_groups_1, items[1], weights, pre)
    total = terms(order_1, *of_groups_1, items[1], grads, total)
    total, got = lax.optimization_barrier((total, got))
    part = lax.psum_scatter(
        total.reshape(TILES, LOCAL * 9 * (C // TILES), C), "tile", scatter_dimension=0, tiled=True
    )
    kernel_grad = part.reshape(LOCAL, 9, C // TILES, C).transpose(0, 1, 3, 2)
    so_far = combine_first(item_slot, got, cotangent)
    out, inner, edges, gate_grad = combine_last(
        item_slot, gates, exchange(rest), frames, cotangent, so_far
    )
    from_below = lax.ppermute(edges[0], "tile", DOWN)
    from_above = lax.ppermute(edges[1], "tile", UP)
    input_grad = (
        inner + from_below.astype(jnp.float32) + from_above.astype(jnp.float32)
    ).astype(jnp.bfloat16)
    return (out[:, None], input_grad[:, None], gate_grad[:, None], kernel_grad)


def solution(mesh):
    return jax.shard_map(
        shards,
        mesh=mesh,
        in_specs=(
            P("dp", "tile", None, None),
            P("dp", None, None, None),
            P("dp", "tile", None),
            P("dp", "tile"),
            P("dp", "tile", None),
            P("dp", "tile", None, None),
        ),
        out_specs=(
            P("dp", "tile", None, None),
            P("dp", "tile", None, None),
            P("dp", "tile", None),
            P("dp", None, None, "tile"),
        ),
        check_vma=False,
    )
```
